128 devices in a mesh: dp: 32 (over z, y, x_hi), tensor: 4 (over x_lo, core).
Axes of the slice: x: 4 (x_hi: 2, x_lo: 2; x = x_hi * 2 + x_lo), y: 4, z: 4, core: 2. Of those that a mesh axis runs over, the one named last changes fastest.
Arguments:
- kv_weight: bfloat16 [32, 512, 16384], P(None, 'dp', 'tensor'), may hold values from -1.5 to 1.5
- momentum: bfloat16 [32, 512, 16384], P(None, 'dp', 'tensor'), may hold values from -36 to 36, as said below
- gradient: bfloat16 [32, 512, 16384], P(None, 'dp', 'tensor'), may hold values from -36 to 36, as said below
- head_counts: int32 [32], replicated, may hold values from 16 to 64, as said below
- logit_peaks: float32 [32, 32, 64], P(None, 'dp', 'tensor'), may hold values from 1.5 to 300, as said below
Outputs:
- update: bfloat16 [32, 512, 16384], P(None, 'dp', 'tensor')
- new_weight: bfloat16 [32, 512, 16384], P(None, 'dp', 'tensor')
- new_momentum: bfloat16 [32, 512, 16384], P(None, 'dp', 'tensor')
The draws below stay inside these ranges and needn't reach their ends.
Inputs may be any that keep to these rules, and one draw needn't show every extreme that they name: momentum: a normal or uniform draw times a row scale and a column scale. gradient: drawn like momentum. `head_counts`: heads 0 to count - 1 of a layer are kept, the others pruned; some layer keeps all 64. `logit_peaks`: positive.
All inputs are finite; a program needn't handle non-finite values.
Results may differ from the reference program's by a relative error of at most 0.015.
The reference program's roundings to bfloat16 on the way count: a program that leaves them out, or rounds other values in their place, can miss the bound.
Values may be sent and summed in bfloat16 or wider, within the bound.
No kernel may reach another device: no remote copies, remote signals or barrier semaphores. Data moves between devices by JAX's collectives and lax.ppermute only.
A program may use at most 128 MiB of HBM per device.

```python
import math
import jax
import jax.numpy as jnp
from jax import lax

LATENT = 512
HEADS = 64
KEY_DIM = 128
VALUE_DIM = 128
ITERS = 5
KV_OUT = 16384
LAYERS = 32
N_DP = 32


def scale_field(key):
    row_key, col_key = jax.random.split(key)
    row_scale = jnp.exp(jax.random.uniform(row_key, (LAYERS, LATENT, 1), jnp.float32, math.log(0.3), math.log(3.0)))
    col_scale = jnp.exp(jax.random.uniform(col_key, (LAYERS, 1, KV_OUT), jnp.float32, math.log(0.3), math.log(3.0)))
    return row_scale * col_scale


def scaled_values(key, scales):
    full_shape = (LAYERS, LATENT, KV_OUT)
    values = jnp.clip(jax.random.normal(key, full_shape, jnp.float32), -4.0, 4.0)
    return (scales * values).astype(jnp.bfloat16)


def draw_momentum(key, part):
    scales = scale_field(key)
    key = jax.random.fold_in(key, 21)
    return scaled_values(key, scales)


def draw_gradient(key, part):
    scales = scale_field(key)
    key = jax.random.fold_in(key, 22)
    return scaled_values(key, scales)


def draw_head_counts(key, part):
    key = jax.random.fold_in(key, 23)
    count_key, pick_key = jax.random.split(key)
    counts = jax.random.randint(count_key, (LAYERS,), HEADS // 4, HEADS + 1)
    chosen = jax.random.randint(pick_key, (), 0, LAYERS)
    return jnp.where(jnp.arange(LAYERS) == chosen, HEADS, counts).astype(jnp.int32)


def draw_logit_peaks(key, part):
    key = jax.random.fold_in(key, 24)
    level_key, spread_key = jax.random.split(key)
    head_level = jnp.exp(jax.random.uniform(level_key, (LAYERS, 1, HEADS), jnp.float32, math.log(30.0), math.log(300.0)))
    spread = jnp.exp(jax.random.uniform(spread_key, (LAYERS, N_DP, HEADS), jnp.float32, math.log(0.05), 0.0))
    return (head_level * spread).astype(jnp.float32)


def steps_of(rng, dims, pieces, smallest, high):
    gain = 1.0
    for dim, parts in pieces:
        draws = jax.random.uniform(jax.random.fold_in(jax.random.fold_in(rng, 6), dim), (parts,), jnp.float32, smallest / len(pieces), high / len(pieces))
        gain = gain * jnp.repeat(jnp.exp(draws), dims[dim] // parts).reshape((-1,) + (1,) * (len(dims) - 1 - dim))
    return gain


def gaussian(key, dims, scale, reach, cuts=(), held_as=jnp.bfloat16):
    gain = steps_of(key, dims, cuts, -0.22, 0.18) if cuts else 1.0
    entries = jax.random.normal(key, dims, jnp.float32) * scale * gain
    return jnp.minimum(jnp.maximum(entries, -reach), reach).astype(held_as)


def setup_inputs(seed: int = 0) -> dict:
    seeds = jax.random.split(jax.random.key(seed), 6)
    return {
        "kv_weight": gaussian(seeds[0], (LAYERS, LATENT, KV_OUT), 0.25, 1.5, ((1, 32), (2, 4))),
        "momentum": draw_momentum(jax.random.fold_in(seeds[5], 71), 0),
        "gradient": draw_gradient(jax.random.fold_in(seeds[5], 71), 0),
        "head_counts": draw_head_counts(jax.random.fold_in(seeds[5], 71), 0),
        "logit_peaks": draw_logit_peaks(jax.random.fold_in(seeds[5], 71), 0),
    }


momentum_decay = 0.95
first_coef = 3.4445
second_coef = -4.775
third_coef = 2.0315
epsilon = 1e-07
clip_limit = 100.0
learn_rate = 0.02
weight_decay = 0.1

def orthogonalize(current):
    norm_scale = None
    for iteration in range(ITERS):
        gram_matrix = jnp.dot(current, current.T, preferred_element_type=jnp.float32)
        if iteration == 0:
            norm_scale = 1.0 / (jnp.sqrt(jnp.trace(gram_matrix)) + epsilon)
            gram_matrix = gram_matrix * norm_scale * norm_scale
        square = jnp.dot(gram_matrix, gram_matrix, precision=lax.Precision.HIGHEST)
        polynomial = (second_coef * gram_matrix + third_coef * square).astype(jnp.bfloat16)
        combined = first_coef * current.astype(jnp.float32) + jnp.dot(polynomial, current, preferred_element_type=jnp.float32)
        if iteration == 0:
            combined = combined * norm_scale
        current = combined.astype(jnp.bfloat16)
    return current

def one_layer(packed):
    weight_rows, moment_rows, grad_rows, count, col_factor = packed
    head_of = jnp.arange(KV_OUT) // (KEY_DIM + VALUE_DIM)
    live_mask = (head_of < count).astype(jnp.float32)
    fresh = (live_mask[None, :] * (momentum_decay * moment_rows.astype(jnp.float32) + grad_rows.astype(jnp.float32))).astype(jnp.bfloat16)
    ortho = orthogonalize(fresh)
    update_scale = 0.2 * math.sqrt(max(LATENT, KV_OUT))
    update = (update_scale * ortho.astype(jnp.float32)).astype(jnp.bfloat16)
    stepped = weight_rows.astype(jnp.float32) * (1.0 - learn_rate * weight_decay) - learn_rate * update.astype(jnp.float32)
    new_weight = (col_factor[None, :] * stepped).astype(jnp.bfloat16)
    return (update, new_weight, fresh)

def reference(kv_weight, momentum, gradient, head_counts, logit_peaks):
    head_peak = lax.optimization_barrier(jnp.max(logit_peaks, axis=1))
    clip_gamma = jnp.minimum(1.0, clip_limit / head_peak)
    key_column = jnp.arange(KV_OUT) % (KEY_DIM + VALUE_DIM) < KEY_DIM
    col_factor = jnp.where(key_column[None, :], jnp.sqrt(jnp.repeat(clip_gamma, KEY_DIM + VALUE_DIM, axis=1)), 1.0)
    update, new_weight, new_momentum = lax.map(one_layer, (kv_weight, momentum, gradient, head_counts, col_factor))
    return (update, new_weight, new_momentum)
```

```python
import math

import jax
import jax.numpy as jnp
from jax import lax
from jax.experimental import pallas as pl
from jax.experimental.pallas import tpu as pltpu
from jax.sharding import PartitionSpec as P

LATENT = 512
KEY_DIM = 128
VALUE_DIM = 128
ITERS = 5
KV_OUT = 16384


momentum_decay = 0.95
first_coef = 3.4445
second_coef = -4.775
third_coef = 2.0315
epsilon = 1e-07
clip_limit = 100.0
learn_rate = 0.02
weight_decay = 0.1

f32 = jnp.float32
bf16 = jnp.bfloat16


def split_two(value):
    high = value.astype(bf16)
    return high, (value - high.astype(f32)).astype(bf16)


def dot(left, right):
    return jnp.dot(left, right, preferred_element_type=f32)


def polynomial_kernel(gram_ref, out_ref):
    gram = gram_ref[...]
    size = gram.shape[0]
    row = lax.broadcasted_iota(jnp.int32, (size, size), 0)
    col = lax.broadcasted_iota(jnp.int32, (size, size), 1)
    diagonal = row == col
    trace = jnp.sum(jnp.where(diagonal, gram, 0.0))
    scale = 1.0 / (jnp.sqrt(trace) + epsilon)
    gram = gram * scale * scale
    total = None
    for iteration in range(ITERS):
        high, low = split_two(gram)
        square = dot(high, high) + (dot(high, low) + dot(low, high))
        poly = (second_coef * gram + third_coef * square).astype(bf16)
        if iteration == 0:
            total = jnp.where(diagonal, first_coef, 0.0) + poly.astype(f32)
        else:
            t_high, t_low = split_two(total)
            total = first_coef * total + (dot(poly, t_high) + dot(poly, t_low))
        if iteration < ITERS - 1:
            half = first_coef * gram + (dot(poly, high) + dot(poly, low))
            h_high, h_low = split_two(half)
            gram = first_coef * half + (dot(h_high, poly) + dot(h_low, poly))
    out_ref[...] = (total * scale).astype(bf16)


def polynomial(gram):
    return pl.pallas_call(
        polynomial_kernel,
        out_shape=jax.ShapeDtypeStruct(gram.shape, bf16),
        in_specs=[pl.BlockSpec(memory_space=pltpu.VMEM)],
        out_specs=pl.BlockSpec(memory_space=pltpu.VMEM),
        compiler_params=pltpu.CompilerParams(vmem_limit_bytes=40 * 2**20),
        cost_estimate=pl.CostEstimate(
            flops=40 * 2 * gram.shape[0] ** 3, bytes_accessed=3 * 2**19, transcendentals=0
        ),
    )(gram)


def scaled_update(owned):
    update_scale = 0.2 * math.sqrt(max(LATENT, KV_OUT))
    local_gram = lax.dot_general(
        owned, owned, (((1,), (1,)), ((), ())), preferred_element_type=f32
    )
    factors = polynomial(lax.psum(local_gram, "tensor"))
    ortho = dot(factors, owned).astype(bf16)
    return (update_scale * ortho.astype(f32)).astype(bf16)


def apply_step(weight_rows, update_rows, col_factor):
    stepped = weight_rows.astype(f32) * (
        1.0 - learn_rate * weight_decay
    ) - learn_rate * update_rows.astype(f32)
    return (col_factor * stepped).astype(bf16)


def on_device(kv_weight, momentum, gradient, head_counts, logit_peaks):
    layers, rows, shard_width = momentum.shape
    head_width = KEY_DIM + VALUE_DIM
    heads_here = shard_width // head_width
    first_head = lax.axis_index("tensor") * heads_here
    head_of = first_head + jnp.arange(shard_width) // head_width
    live_mask = (head_of[None, :] < head_counts[:, None]).astype(f32)
    new_momentum = (
        live_mask[:, None, :]
        * (momentum_decay * momentum.astype(f32) + gradient.astype(f32))
    ).astype(bf16)
    head_peak = jnp.max(lax.all_gather(logit_peaks[:, 0, :], "dp"), axis=0)
    clip_gamma = jnp.minimum(1.0, clip_limit / head_peak)
    key_column = jnp.arange(shard_width) % head_width < KEY_DIM
    col_factor = jnp.where(
        key_column[None, :], jnp.sqrt(jnp.repeat(clip_gamma, head_width, axis=1)), 1.0
    )
    owned = lax.all_to_all(new_momentum, "dp", split_axis=0, concat_axis=0, tiled=True)
    owned_update = scaled_update(owned.reshape(layers * rows, shard_width))
    update = lax.all_to_all(
        owned_update.reshape(layers, rows, shard_width),
        "dp",
        split_axis=0,
        concat_axis=0,
        tiled=True,
    )
    new_weight = apply_step(kv_weight, update, col_factor[:, None, :])
    return (update, new_weight, new_momentum)


def solution(mesh):
    placed = (
        P(None, "dp", "tensor"),
        P(None, "dp", "tensor"),
        P(None, "dp", "tensor"),
        P(),
        P(None, "dp", "tensor"),
    )
    return jax.shard_map(
        on_device,
        mesh=mesh,
        in_specs=placed,
        out_specs=(P(None, "dp", "tensor"), P(None, "dp", "tensor"), P(None, "dp", "tensor")),
        check_vma=False,
    )
```

```python
import functools
import math

import jax
import jax.numpy as jnp
from jax import lax
from jax.experimental import pallas as pl
from jax.experimental.pallas import tpu as pltpu
from jax.sharding import PartitionSpec as P

LATENT = 512
KEY_DIM = 128
VALUE_DIM = 128
ITERS = 5
KV_OUT = 16384


momentum_decay = 0.95
first_coef = 3.4445
second_coef = -4.775
third_coef = 2.0315
epsilon = 1e-07
clip_limit = 100.0
learn_rate = 0.02
weight_decay = 0.1

f32 = jnp.float32
bf16 = jnp.bfloat16
MIB = 2**20
TILE = 128
GR = 256
HALF = GR * 3 // 2
VMEM = pl.BlockSpec(memory_space=pltpu.VMEM)
SMEM = pl.BlockSpec(memory_space=pltpu.SMEM)
HBM = pl.BlockSpec(memory_space=pltpu.HBM)


def dot(left, right):
    return jnp.dot(left, right, preferred_element_type=f32)


def dot_nt(left, right):
    return lax.dot_general(left, right, (((1,), (1,)), ((), ())), preferred_element_type=f32)


def eye_tile():
    shape = (TILE, TILE)
    return lax.broadcasted_iota(jnp.int32, shape, 0) == lax.broadcasted_iota(jnp.int32, shape, 1)


def tiles_of(ref):
    return [pl.ds(i * TILE, TILE) for i in range(ref.shape[0] // TILE)]


def gram_kernel(core_ref, x_ref, keep_ref, give_ref):
    top = x_ref[0:GR, :]
    bottom = x_ref[GR:, :]
    parts = (dot_nt(top, top), dot_nt(top, bottom), dot_nt(bottom, bottom))
    for core, (low, high) in enumerate(((keep_ref, give_ref), (give_ref, keep_ref))):

        @pl.when(core_ref[0] == core)
        def _():
            low[0:GR, :] = parts[0]
            low[GR:, :] = parts[1][0 : GR // 2]
            high[0:GR, :] = parts[2]
            high[GR:, :] = parts[1][GR // 2 :]


def gram_halves(core, x):
    rows, cols = x.shape
    half = jax.ShapeDtypeStruct((HALF, GR), f32)
    return pl.pallas_call(
        gram_kernel,
        out_shape=(half, half),
        in_specs=[SMEM, VMEM],
        out_specs=(VMEM, VMEM),
        compiler_params=pltpu.CompilerParams(vmem_limit_bytes=32 * MIB),
        cost_estimate=pl.CostEstimate(
            flops=rows * rows * cols * 3 // 2, bytes_accessed=rows * cols * 2, transcendentals=0
        ),
    )(core, x)


def split_diagonal(full_ref, off_ref):
    eye = eye_tile()
    off_ref[...] = full_ref[...].astype(bf16)
    rows, cols = [], []
    for at in tiles_of(full_ref):
        tile = full_ref[at, at].astype(f32)
        on = jnp.where(eye, tile, 0.0)
        off_ref[at, at] = jnp.where(eye, 0.0, tile).astype(bf16)
        rows.append(jnp.sum(on, axis=0, keepdims=True))
        cols.append(jnp.sum(on, axis=1, keepdims=True))
    return jnp.concatenate(rows, 1), jnp.concatenate(cols, 0)


def less_diagonal(ref, col, row):
    eye = eye_tile()
    for i, at in enumerate(tiles_of(ref)):
        span = slice(i * TILE, (i + 1) * TILE)
        ref[at, at] = ref[at, at] - jnp.where(eye, col[span] * row[:, span], 0.0)


def newton_schulz(gram, half, total, poly, gram_off, half_off, total_off, poly_off):
    eye = eye_tile()
    trace = 0.0
    for at in tiles_of(gram):
        trace = trace + jnp.sum(jnp.where(eye, gram[at, at], 0.0))
    scale = 1.0 / (jnp.sqrt(trace) + epsilon)
    gram[...] = gram[...] * scale * scale
    for iteration in range(ITERS):
        g_row, g_col = split_diagonal(gram, gram_off)
        half[...] = third_coef * dot(gram_off[...], gram_off[...]) + gram[...] * (
            second_coef + third_coef * (g_col + g_row)
        )
        less_diagonal(half, third_coef * g_col, g_row)
        poly[...] = half[...].astype(bf16)
        p_row, p_col = split_diagonal(poly, poly_off)
        if iteration == 0:
            total[...] = poly[...].astype(f32)
            for at in tiles_of(total):
                total[at, at] = total[at, at] + jnp.where(eye, first_coef, 0.0)
        else:
            t_row, t_col = split_diagonal(total, total_off)
            total[...] = (
                dot(poly_off[...], total_off[...])
                + (first_coef + p_col) * total[...]
                + poly[...].astype(f32) * t_row
            )
            less_diagonal(total, p_col, t_row)
        if iteration < ITERS - 1:
            half[...] = (
                dot(poly_off[...], gram_off[...])
                + (first_coef + p_col) * gram[...]
                + poly[...].astype(f32) * g_row
            )
            less_diagonal(half, p_col, g_row)
            h_row, h_col = split_diagonal(half, half_off)
            gram[...] = (
                dot(half_off[...], poly_off[...])
                + half[...] * (first_coef + p_row)
                + h_col * poly[...].astype(f32)
            )
            less_diagonal(gram, h_col, p_row)
    return scale


def peak_block(peak):
    high = peak.astype(bf16).astype(f32)
    rest = peak - high
    middle = rest.astype(bf16).astype(f32)
    low = (rest - middle).astype(bf16).astype(f32)
    return (high + pltpu.roll(middle, 32, 1) + pltpu.roll(low, 64, 1)).astype(bf16)


def update_kernel(
    update_scale, width, rows_here,
    core_ref, mine_ref, other_ref, peak_ref, x_ref, weight_hbm, out_ref, weight_ref,
    gram, half, total, poly, gram_off, half_off, total_off, poly_off, factors, weight_sem,
):
    fetch = pltpu.make_async_copy(weight_hbm, weight_ref, weight_sem)
    fetch.start()
    for core, (low, high) in enumerate(((mine_ref, other_ref), (other_ref, mine_ref))):

        @pl.when(core_ref[0] == core)
        def _():
            gram[0:GR, 0:GR] = low[0:GR, :]
            gram[GR:, GR:] = high[0:GR, :]
            cross = jnp.concatenate([low[GR:, :], high[GR:, :]], 0)
            gram[0:GR, GR:] = cross
            gram[GR:, 0:GR] = cross.T

    scale = newton_schulz(
        gram, half, total, poly, gram_off, half_off, total_off, poly_off
    )
    factors[...] = (total[...] * scale).astype(bf16)
    rows, cols = x_ref.shape

    @pl.loop(0, cols // width)
    def _(step):
        at = pl.ds(pl.multiple_of(step * width, width), width)
        ortho = dot(factors[...], x_ref[:, at]).astype(bf16)
        out_ref[:, at] = (update_scale * ortho.astype(f32)).astype(bf16)

    block = peak_block(peak_ref[...])
    for i in range(rows // rows_here):
        out_ref[pl.ds(i * rows_here, rows_here), pl.ds(cols, TILE)] = block
    fetch.wait()


def scaled_update(core, mine, other, peak, x, kv_weight):
    rows, cols = x.shape
    square = (rows, rows)
    return pl.pallas_call(
        functools.partial(
            update_kernel, 0.2 * math.sqrt(max(LATENT, KV_OUT)), 1024, kv_weight.shape[1]
        ),
        out_shape=(
            jax.ShapeDtypeStruct((rows, cols + TILE), bf16),
            jax.ShapeDtypeStruct(kv_weight.shape, bf16),
        ),
        in_specs=[SMEM, VMEM, VMEM, VMEM, VMEM, HBM],
        out_specs=(VMEM, VMEM),
        scratch_shapes=[pltpu.VMEM(square, f32)] * 3
        + [pltpu.VMEM(square, bf16)] * 6
        + [pltpu.SemaphoreType.DMA],
        compiler_params=pltpu.CompilerParams(vmem_limit_bytes=45 * MIB),
        cost_estimate=pl.CostEstimate(
            flops=34 * rows**3 + 2 * rows * rows * cols,
            bytes_accessed=rows * cols * 4,
            transcendentals=0,
        ),
    )(core, mine, other, peak, x, kv_weight)


def gram_sum(core, x):
    other_core = [(i, i ^ 1) for i in range(4)]
    other_chip = [(i, i ^ 2) for i in range(4)]
    keep, give = gram_halves(core, x)
    mine = keep + lax.ppermute(give, "tensor", other_core)
    mine = mine + lax.ppermute(mine, "tensor", other_chip)
    return mine, lax.ppermute(mine, "tensor", other_core)


def step_kernel(weight_ref, recv_ref, update_hbm, new_ref, factor_ref, update_sem):
    step = pl.program_id(0)
    layers, rows, cols = weight_ref.shape
    group = new_ref.shape[0]
    store = pltpu.make_async_copy(recv_ref.at[:, :, pl.ds(0, cols)], update_hbm, update_sem)

    @pl.when(step == 0)
    def _():
        store.start()
        parts = recv_ref[:, :, pl.ds(cols, TILE)].astype(f32)
        peak = None
        for i in range(layers):
            high = parts[i]
            joined = high + pltpu.roll(high, TILE - 32, 1) + pltpu.roll(high, TILE - 64, 1)
            peak = joined if peak is None else jnp.maximum(peak, joined)
        factor_ref[...] = jnp.sqrt(jnp.minimum(1.0, clip_limit / peak))

    heads = cols // (2 * TILE)
    lane = lax.broadcasted_iota(jnp.int32, factor_ref.shape, 1)
    for i in range(group):
        layer = step * group + i
        factors = jnp.sum(jnp.where(lane == layer, factor_ref[...], 0.0), axis=1, keepdims=True)
        for head in range(heads):
            for part in range(2):
                at = pl.ds((2 * head + part) * TILE, TILE)
                stepped = weight_ref[layer, :, at].astype(f32) * (
                    1.0 - learn_rate * weight_decay
                ) - learn_rate * recv_ref[layer, :, at].astype(f32)
                if part == 0:
                    stepped = factors[head : head + 1, :] * stepped
                new_ref[i, :, at] = stepped.astype(bf16)

    @pl.when(step == pl.num_programs(0) - 1)
    def _():
        store.wait()


def apply_step(kv_weight, received):
    layers, rows, cols = kv_weight.shape
    group = layers // 4
    shape = jax.ShapeDtypeStruct(kv_weight.shape, bf16)
    return pl.pallas_call(
        step_kernel,
        grid=(layers // group,),
        out_shape=(shape, shape),
        in_specs=[VMEM, VMEM],
        out_specs=(
            pl.BlockSpec(memory_space=pl.ANY),
            pl.BlockSpec((group, rows, cols), lambda i: (i, 0, 0)),
        ),
        scratch_shapes=[pltpu.VMEM((rows, TILE), f32), pltpu.SemaphoreType.DMA],
        compiler_params=pltpu.CompilerParams(vmem_limit_bytes=24 * MIB),
        cost_estimate=pl.CostEstimate(
            flops=4 * layers * rows * cols, bytes_accessed=8 * layers * rows * cols, transcendentals=0
        ),
    )(kv_weight, received)


def on_device(kv_weight, momentum, gradient, head_counts, logit_peaks):
    layers, rows, shard_width = momentum.shape
    heads_here = shard_width // (KEY_DIM + VALUE_DIM)
    tensor_index = lax.axis_index("tensor")
    core = (tensor_index % 2).astype(jnp.int32).reshape(1)
    head_of = tensor_index * heads_here + jnp.arange(shard_width) // (KEY_DIM + VALUE_DIM)
    live_mask = (head_of[None, :] < head_counts[:, None]).astype(f32)
    new_momentum = (
        live_mask[:, None, :]
        * (momentum_decay * momentum.astype(f32) + gradient.astype(f32))
    ).astype(bf16)
    peaks = jnp.pad(logit_peaks[:, 0, :].T, ((0, 0), (0, TILE - layers)))
    new_momentum, peaks, core = lax.optimization_barrier((new_momentum, peaks, core))
    owned = lax.all_to_all(new_momentum, "dp", split_axis=0, concat_axis=0, tiled=True)
    owned = owned.reshape(layers * rows, shard_width)
    mine, other = gram_sum(core, owned)
    owned_update, weight = scaled_update(
        core, mine, other, peaks, owned, kv_weight
    )
    received = lax.all_to_all(
        owned_update.reshape(layers, rows, shard_width + TILE),
        "dp",
        split_axis=0,
        concat_axis=0,
        tiled=True,
    )
    update, new_weight = apply_step(weight, received)
    return (update, new_weight, new_momentum)


def solution(mesh):
    placed = (
        P(None, "dp", "tensor"),
        P(None, "dp", "tensor"),
        P(None, "dp", "tensor"),
        P(),
        P(None, "dp", "tensor"),
    )
    return jax.shard_map(
        on_device,
        mesh=mesh,
        in_specs=placed,
        out_specs=(P(None, "dp", "tensor"), P(None, "dp", "tensor"), P(None, "dp", "tensor")),
        check_vma=False,
    )
```

```python
import functools
import math

import jax
import jax.numpy as jnp
from jax import lax
from jax.experimental import pallas as pl
from jax.experimental.pallas import tpu as pltpu
from jax.sharding import PartitionSpec as P

LATENT = 512
KEY_DIM = 128
VALUE_DIM = 128
ITERS = 5
KV_OUT = 16384


momentum_decay = 0.95
first_coef = 3.4445
second_coef = -4.775
third_coef = 2.0315
epsilon = 1e-07
clip_limit = 100.0
learn_rate = 0.02
weight_decay = 0.1

f32 = jnp.float32
bf16 = jnp.bfloat16
MIB = 2**20
TILE = 128
GR = 256
HALF = 4 * TILE + 8
VMEM = pl.BlockSpec(memory_space=pltpu.VMEM)
SMEM = pl.BlockSpec(memory_space=pltpu.SMEM)
HBM = pl.BlockSpec(memory_space=pltpu.HBM)


def dot(left, right):
    return jnp.dot(left, right, preferred_element_type=f32)


def dot_nt(left, right):
    return lax.dot_general(left, right, (((1,), (1,)), ((), ())), preferred_element_type=f32)


def eye_tile():
    shape = (TILE, TILE)
    return lax.broadcasted_iota(jnp.int32, shape, 0) == lax.broadcasted_iota(jnp.int32, shape, 1)


def tiles_of(ref):
    return [pl.ds(i * TILE, TILE) for i in range(ref.shape[0] // TILE)]


def pack_half(half_ref, square, across):
    row = lax.broadcasted_iota(jnp.int32, (TILE, TILE), 0)
    col = lax.broadcasted_iota(jnp.int32, (TILE, TILE), 1)
    first, second = square[:TILE, :TILE], square[TILE:, TILE:]
    half_ref[pl.ds(0, TILE), :] = jnp.where(row <= col, first, second)
    half_ref[pl.ds(TILE, TILE), :] = square[:TILE, TILE:]
    half_ref[pl.ds(2 * TILE, TILE), :] = across[:, :TILE]
    half_ref[pl.ds(3 * TILE, TILE), :] = across[:, TILE:]
    diagonal = jnp.sum(jnp.where(row == col, second, 0.0), axis=0, keepdims=True)
    half_ref[pl.ds(4 * TILE, 8), :] = jnp.broadcast_to(diagonal, (8, TILE))


def unpack_half(half_ref, gram, which):
    row = lax.broadcasted_iota(jnp.int32, (TILE, TILE), 0)
    col = lax.broadcasted_iota(jnp.int32, (TILE, TILE), 1)

    def put(i, j, tile):
        gram[pl.ds(i * TILE, TILE), pl.ds(j * TILE, TILE)] = tile

    both = half_ref[pl.ds(0, TILE), :]
    turned = both.T
    base = 2 * which
    put(base, base, jnp.where(row <= col, both, turned))
    second = jnp.where(row > col, both, turned)
    put(base + 1, base + 1, jnp.where(row == col, half_ref[pl.ds(4 * TILE, 1), :], second))
    for k, (i, j) in enumerate(((base, base + 1), (which, 2), (which, 3))):
        tile = half_ref[pl.ds((k + 1) * TILE, TILE), :]
        put(i, j, tile)
        put(j, i, tile.T)


def gram_kernel(own, core_ref, x_ref, half_ref):
    for which in range(2):

        @pl.when(core_ref[0] == (which if own else 1 - which))
        def _():
            block = x_ref[pl.ds(which * GR, GR), :]
            band = x_ref[pl.ds(which * TILE, TILE), :]
            pack_half(half_ref, dot_nt(block, block), dot_nt(band, x_ref[pl.ds(GR, GR), :]))


def gram_half(own, core, x):
    rows, cols = x.shape
    return pl.pallas_call(
        functools.partial(gram_kernel, own),
        out_shape=jax.ShapeDtypeStruct((HALF, TILE), f32),
        in_specs=[SMEM, VMEM],
        out_specs=VMEM,
        compiler_params=pltpu.CompilerParams(vmem_limit_bytes=32 * MIB),
        cost_estimate=pl.CostEstimate(
            flops=rows * rows * cols * 3 // 4, bytes_accessed=rows * cols * 2, transcendentals=0
        ),
    )(core, x)


def to_col(row):
    tiles = [row[:, i : i + TILE] for i in range(0, row.shape[1], TILE)]
    return jnp.concatenate([jnp.broadcast_to(t, (8, TILE)).T[:, 0:1] for t in tiles], 0)


def settle(value, extra, full_ref, off_ref):
    eye = eye_tile()
    kind = full_ref.dtype
    full_ref[...] = value.astype(kind)
    off_ref[...] = value.astype(bf16)
    found = []
    for i in range(0, value.shape[0], TILE):
        at = pl.ds(i, TILE)
        tile = value[i : i + TILE, i : i + TILE]
        row = jnp.sum(jnp.where(eye, tile, 0.0), axis=0, keepdims=True)
        if extra is not None:
            row = row - extra[:, i : i + TILE]
        if kind != f32:
            row = row.astype(kind).astype(f32)
        full_ref[at, at] = jnp.where(eye, row, tile).astype(kind)
        off_ref[at, at] = jnp.where(eye, 0.0, tile).astype(bf16)
        found.append(row)
    return jnp.concatenate(found, 1)


def newton_schulz(gram, half, total, poly, gram_off, half_off, total_off, poly_off):
    eye = eye_tile()
    trace = 0.0
    for at in tiles_of(gram):
        trace = trace + jnp.sum(jnp.where(eye, gram[at, at], 0.0))
    scale = 1.0 / (jnp.sqrt(trace) + epsilon)
    g_row = settle(gram[...] * scale * scale, None, gram, gram_off)
    for iteration in range(ITERS):
        g_col = to_col(g_row)
        square = third_coef * dot(gram_off[...], gram_off[...])
        p_row = settle(
            square + gram[...] * (second_coef + third_coef * (g_col + g_row)),
            third_coef * g_row * g_row,
            poly,
            poly_off,
        )
        p_col = to_col(p_row)
        if iteration < ITERS - 1:
            h_row = settle(
                dot(poly_off[...], gram_off[...])
                + (first_coef + p_col) * gram[...]
                + poly[...].astype(f32) * g_row,
                p_row * g_row,
                half,
                half_off,
            )
        if iteration == 0:
            t_row = settle(poly[...].astype(f32), jnp.full_like(p_row, -first_coef), total, total_off)
        else:
            t_row = settle(
                dot(poly_off[...], total_off[...])
                + (first_coef + p_col) * total[...]
                + poly[...].astype(f32) * t_row,
                p_row * t_row,
                total,
                total_off,
            )
        if iteration < ITERS - 1:
            g_row = settle(
                dot(half_off[...], poly_off[...])
                + half[...] * (first_coef + p_row)
                + to_col(h_row) * poly[...].astype(f32),
                h_row * p_row,
                gram,
                gram_off,
            )
    return scale


def peak_block(peak):
    high = peak.astype(bf16).astype(f32)
    rest = peak - high
    middle = rest.astype(bf16).astype(f32)
    low = (rest - middle).astype(bf16).astype(f32)
    return (high + pltpu.roll(middle, 32, 1) + pltpu.roll(low, 64, 1)).astype(bf16)


def update_kernel(
    update_scale, width, rows_here,
    core_ref, mine_ref, other_ref, peak_ref, x_ref, weight_hbm, out_ref, weight_ref,
    gram, half, total, poly, gram_off, half_off, total_off, poly_off, factors, weight_sem,
):
    fetch = pltpu.make_async_copy(weight_hbm, weight_ref, weight_sem)
    fetch.start()
    for core, halves in enumerate(((mine_ref, other_ref), (other_ref, mine_ref))):

        @pl.when(core_ref[0] == core)
        def _():
            for which, half_ref in enumerate(halves):
                unpack_half(half_ref, gram, which)

    scale = newton_schulz(
        gram, half, total, poly, gram_off, half_off, total_off, poly_off
    )
    factors[...] = (total[...] * scale).astype(bf16)
    rows, cols = x_ref.shape

    for start in range(0, cols, width):
        at = pl.ds(start, width)
        ortho = dot(factors[...], x_ref[:, at]).astype(bf16)
        out_ref[:, at] = (update_scale * ortho.astype(f32)).astype(bf16)

    block = peak_block(peak_ref[...])
    for i in range(rows // rows_here):
        out_ref[pl.ds(i * rows_here, rows_here), pl.ds(cols, TILE)] = block
    fetch.wait()


def scaled_update(core, mine, other, peak, x, kv_weight):
    rows, cols = x.shape
    square = (rows, rows)
    return pl.pallas_call(
        functools.partial(
            update_kernel, 0.2 * math.sqrt(max(LATENT, KV_OUT)), 1024, kv_weight.shape[1]
        ),
        out_shape=(
            jax.ShapeDtypeStruct((rows, cols + TILE), bf16),
            jax.ShapeDtypeStruct(kv_weight.shape, bf16),
        ),
        in_specs=[SMEM, VMEM, VMEM, VMEM, VMEM, HBM],
        out_specs=(VMEM, VMEM),
        scratch_shapes=[pltpu.VMEM(square, f32)] * 3
        + [pltpu.VMEM(square, bf16)] * 6
        + [pltpu.SemaphoreType.DMA],
        compiler_params=pltpu.CompilerParams(vmem_limit_bytes=45 * MIB),
        cost_estimate=pl.CostEstimate(
            flops=34 * rows**3 + 2 * rows * rows * cols,
            bytes_accessed=rows * cols * 4,
            transcendentals=0,
        ),
    )(core, mine, other, peak, x, kv_weight)


def gram_sum(core, x, peaks):
    other_core = [(i, i ^ 1) for i in range(4)]
    other_chip = [(i, i ^ 2) for i in range(4)]
    given = lax.ppermute(gram_half(False, core, x), "tensor", other_core)
    mine = gram_half(True, core, x) + given
    mine, peaks = lax.optimization_barrier((mine, peaks))
    peaks = jnp.pad(peaks, ((0, 0), (0, TILE - peaks.shape[1])))
    mine = mine + lax.ppermute(mine, "tensor", other_chip)
    mine, peaks = lax.optimization_barrier((mine, peaks))
    return mine, lax.ppermute(mine, "tensor", other_core), peaks


def step_kernel(weight_ref, recv_ref, update_hbm, new_ref, factor_ref, update_sem):
    step = pl.program_id(0)
    layers, rows, cols = weight_ref.shape
    group = new_ref.shape[0]
    store = pltpu.make_async_copy(recv_ref.at[:, :, pl.ds(0, cols)], update_hbm, update_sem)

    @pl.when(step == 0)
    def _():
        store.start()
        parts = recv_ref[:, :, pl.ds(cols, TILE)].astype(f32)
        peak = None
        for i in range(layers):
            high = parts[i]
            joined = high + pltpu.roll(high, TILE - 32, 1) + pltpu.roll(high, TILE - 64, 1)
            peak = joined if peak is None else jnp.maximum(peak, joined)
        factor_ref[...] = jnp.sqrt(jnp.minimum(1.0, clip_limit / peak))

    heads = cols // (2 * TILE)
    lane = lax.broadcasted_iota(jnp.int32, factor_ref.shape, 1)
    for i in range(group):
        layer = step * group + i
        factors = jnp.sum(jnp.where(lane == layer, factor_ref[...], 0.0), axis=1, keepdims=True)
        for head in range(heads):
            for part in range(2):
                at = pl.ds((2 * head + part) * TILE, TILE)
                stepped = weight_ref[layer, :, at].astype(f32) * (
                    1.0 - learn_rate * weight_decay
                ) - learn_rate * recv_ref[layer, :, at].astype(f32)
                if part == 0:
                    stepped = factors[head : head + 1, :] * stepped
                new_ref[i, :, at] = stepped.astype(bf16)

    @pl.when(step == pl.num_programs(0) - 1)
    def _():
        store.wait()


def apply_step(kv_weight, received):
    layers, rows, cols = kv_weight.shape
    group = layers // 4
    shape = jax.ShapeDtypeStruct(kv_weight.shape, bf16)
    return pl.pallas_call(
        step_kernel,
        grid=(layers // group,),
        out_shape=(shape, shape),
        in_specs=[VMEM, VMEM],
        out_specs=(
            pl.BlockSpec(memory_space=pl.ANY),
            pl.BlockSpec((group, rows, cols), lambda i: (i, 0, 0)),
        ),
        scratch_shapes=[pltpu.VMEM((rows, TILE), f32), pltpu.SemaphoreType.DMA],
        compiler_params=pltpu.CompilerParams(vmem_limit_bytes=24 * MIB),
        cost_estimate=pl.CostEstimate(
            flops=4 * layers * rows * cols, bytes_accessed=8 * layers * rows * cols, transcendentals=0
        ),
    )(kv_weight, received)


def on_device(kv_weight, momentum, gradient, head_counts, logit_peaks):
    layers, rows, shard_width = momentum.shape
    heads_here = shard_width // (KEY_DIM + VALUE_DIM)
    tensor_index = lax.axis_index("tensor")
    core = (tensor_index % 2).astype(jnp.int32).reshape(1)
    head_of = tensor_index * heads_here + lax.broadcasted_iota(
        jnp.int32, momentum.shape, 2
    ) // (KEY_DIM + VALUE_DIM)
    live_mask = (head_of < head_counts[:, None, None]).astype(f32)
    new_momentum = (
        live_mask
        * (momentum_decay * momentum.astype(f32) + gradient.astype(f32))
    ).astype(bf16)
    new_momentum, core = lax.optimization_barrier((new_momentum, core))
    owned = lax.all_to_all(new_momentum, "dp", split_axis=0, concat_axis=0, tiled=True)
    owned = owned.reshape(layers * rows, shard_width)
    mine, other, peaks = gram_sum(core, owned, logit_peaks[:, 0, :].T)
    owned_update, weight = scaled_update(
        core, mine, other, peaks, owned, kv_weight
    )
    received = lax.all_to_all(
        owned_update.reshape(layers, rows, shard_width + TILE),
        "dp",
        split_axis=0,
        concat_axis=0,
        tiled=True,
    )
    update, new_weight = apply_step(weight, received)
    return (update, new_weight, new_momentum)


def solution(mesh):
    placed = (
        P(None, "dp", "tensor"),
        P(None, "dp", "tensor"),
        P(None, "dp", "tensor"),
        P(),
        P(None, "dp", "tensor"),
    )
    return jax.shard_map(
        on_device,
        mesh=mesh,
        in_specs=placed,
        out_specs=(P(None, "dp", "tensor"), P(None, "dp", "tensor"), P(None, "dp", "tensor")),
        check_vma=False,
    )
```

```python
import functools
import math

import jax
import jax.numpy as jnp
from jax import lax
from jax.experimental import pallas as pl
from jax.experimental.pallas import tpu as pltpu
from jax.sharding import PartitionSpec as P

LATENT = 512
KEY_DIM = 128
VALUE_DIM = 128
ITERS = 5
KV_OUT = 16384


momentum_decay = 0.95
first_coef = 3.4445
second_coef = -4.775
third_coef = 2.0315
epsilon = 1e-07
clip_limit = 100.0
learn_rate = 0.02
weight_decay = 0.1

f32 = jnp.float32
bf16 = jnp.bfloat16
MIB = 2**20
TILE = 128
GR = 256
HALF = 4 * TILE + 8
VMEM = pl.BlockSpec(memory_space=pltpu.VMEM)
SMEM = pl.BlockSpec(memory_space=pltpu.SMEM)
HBM = pl.BlockSpec(memory_space=pltpu.HBM)


def dot(left, right):
    return jnp.dot(left, right, preferred_element_type=f32)


def dot_nt(left, right):
    return lax.dot_general(left, right, (((1,), (1,)), ((), ())), preferred_element_type=f32)


def eye_tile():
    shape = (TILE, TILE)
    return lax.broadcasted_iota(jnp.int32, shape, 0) == lax.broadcasted_iota(jnp.int32, shape, 1)


def tiles_of(ref):
    return [pl.ds(i * TILE, TILE) for i in range(ref.shape[0] // TILE)]


def pack_half(half_ref, square, across):
    row = lax.broadcasted_iota(jnp.int32, (TILE, TILE), 0)
    col = lax.broadcasted_iota(jnp.int32, (TILE, TILE), 1)
    first, second = square[:TILE, :TILE], square[TILE:, TILE:]
    half_ref[pl.ds(0, TILE), :] = jnp.where(row <= col, first, second)
    half_ref[pl.ds(TILE, TILE), :] = square[:TILE, TILE:]
    half_ref[pl.ds(2 * TILE, TILE), :] = across[:, :TILE]
    half_ref[pl.ds(3 * TILE, TILE), :] = across[:, TILE:]
    diagonal = jnp.sum(jnp.where(row == col, second, 0.0), axis=0, keepdims=True)
    half_ref[pl.ds(4 * TILE, 8), :] = jnp.broadcast_to(diagonal, (8, TILE))


def unpack_half(half_ref, gram, which):
    row = lax.broadcasted_iota(jnp.int32, (TILE, TILE), 0)
    col = lax.broadcasted_iota(jnp.int32, (TILE, TILE), 1)

    def put(i, j, tile):
        gram[pl.ds(i * TILE, TILE), pl.ds(j * TILE, TILE)] = tile

    both = half_ref[pl.ds(0, TILE), :]
    turned = both.T
    base = 2 * which
    put(base, base, jnp.where(row <= col, both, turned))
    second = jnp.where(row > col, both, turned)
    put(base + 1, base + 1, jnp.where(row == col, half_ref[pl.ds(4 * TILE, 1), :], second))
    for k, (i, j) in enumerate(((base, base + 1), (which, 2), (which, 3))):
        tile = half_ref[pl.ds((k + 1) * TILE, TILE), :]
        put(i, j, tile)
        put(j, i, tile.T)


def gram_kernel(own, core_ref, x_ref, half_ref):
    for which in range(2):

        @pl.when(core_ref[0] == (which if own else 1 - which))
        def _():
            block = x_ref[pl.ds(which * GR, GR), :]
            band = x_ref[pl.ds(which * TILE, TILE), :]
            pack_half(half_ref, dot_nt(block, block), dot_nt(band, x_ref[pl.ds(GR, GR), :]))


def gram_half(own, core, x):
    rows, cols = x.shape
    return pl.pallas_call(
        functools.partial(gram_kernel, own),
        out_shape=jax.ShapeDtypeStruct((HALF, TILE), f32),
        in_specs=[SMEM, VMEM],
        out_specs=VMEM,
        compiler_params=pltpu.CompilerParams(vmem_limit_bytes=32 * MIB),
        cost_estimate=pl.CostEstimate(
            flops=rows * rows * cols * 3 // 4, bytes_accessed=rows * cols * 2, transcendentals=0
        ),
    )(core, x)


def to_col(row):
    tiles = [row[:, i : i + TILE] for i in range(0, row.shape[1], TILE)]
    return jnp.concatenate([jnp.broadcast_to(t, (8, TILE)).T[:, 0:1] for t in tiles], 0)


def settle(value, extra, full_ref, off_ref):
    eye = eye_tile()
    kind = full_ref.dtype
    full_ref[...] = value.astype(kind)
    off_ref[...] = value.astype(bf16)
    found = []
    for i in range(0, value.shape[0], TILE):
        at = pl.ds(i, TILE)
        tile = value[i : i + TILE, i : i + TILE]
        row = jnp.sum(jnp.where(eye, tile, 0.0), axis=0, keepdims=True)
        if extra is not None:
            row = row - extra[:, i : i + TILE]
        if kind != f32:
            row = row.astype(kind).astype(f32)
        full_ref[at, at] = jnp.where(eye, row, tile).astype(kind)
        off_ref[at, at] = jnp.where(eye, 0.0, tile).astype(bf16)
        found.append(row)
    return jnp.concatenate(found, 1)


def newton_schulz(gram, half, total, poly, gram_off, half_off, total_off, poly_off):
    eye = eye_tile()
    trace = 0.0
    for at in tiles_of(gram):
        trace = trace + jnp.sum(jnp.where(eye, gram[at, at], 0.0))
    scale = 1.0 / (jnp.sqrt(trace) + epsilon)
    g_row = settle(gram[...] * scale * scale, None, gram, gram_off)
    for iteration in range(ITERS):
        g_col = to_col(g_row)
        square = third_coef * dot(gram_off[...], gram_off[...])
        p_row = settle(
            square + gram[...] * (second_coef + third_coef * (g_col + g_row)),
            third_coef * g_row * g_row,
            poly,
            poly_off,
        )
        p_col = to_col(p_row)
        if iteration < ITERS - 1:
            h_row = settle(
                dot(poly_off[...], gram_off[...])
                + (first_coef + p_col) * gram[...]
                + poly[...].astype(f32) * g_row,
                p_row * g_row,
                half,
                half_off,
            )
        if iteration == 0:
            t_row = settle(poly[...].astype(f32), jnp.full_like(p_row, -first_coef), total, total_off)
        else:
            t_row = settle(
                dot(poly_off[...], total_off[...])
                + (first_coef + p_col) * total[...]
                + poly[...].astype(f32) * t_row,
                p_row * t_row,
                total,
                total_off,
            )
        if iteration < ITERS - 1:
            g_row = settle(
                dot(half_off[...], poly_off[...])
                + half[...] * (first_coef + p_row)
                + to_col(h_row) * poly[...].astype(f32),
                h_row * p_row,
                gram,
                gram_off,
            )
    return scale


def peak_block(peak):
    high = peak.astype(bf16).astype(f32)
    rest = peak - high
    middle = rest.astype(bf16).astype(f32)
    low = (rest - middle).astype(bf16).astype(f32)
    return (high + pltpu.roll(middle, 32, 1) + pltpu.roll(low, 64, 1)).astype(bf16)


def update_kernel(
    update_scale, width, rows_here,
    core_ref, mine_ref, other_ref, peak_ref, x_ref, weight_hbm, out_ref, weight_ref,
    gram, half, total, poly, gram_off, half_off, total_off, poly_off, factors, weight_sem,
):
    fetch = pltpu.make_async_copy(weight_hbm, weight_ref, weight_sem)
    fetch.start()
    for core, halves in enumerate(((mine_ref, other_ref), (other_ref, mine_ref))):

        @pl.when(core_ref[0] == core)
        def _():
            for which, half_ref in enumerate(halves):
                unpack_half(half_ref, gram, which)

    scale = newton_schulz(
        gram, half, total, poly, gram_off, half_off, total_off, poly_off
    )
    factors[...] = (total[...] * scale).astype(bf16)
    rows, cols = x_ref.shape

    for start in range(0, cols, width):
        at = pl.ds(start, width)
        ortho = dot(factors[...], x_ref[:, at]).astype(bf16)
        out_ref[:, at] = (update_scale * ortho.astype(f32)).astype(bf16)

    block = peak_block(peak_ref[...])
    for i in range(rows // rows_here):
        out_ref[pl.ds(i * rows_here, rows_here), pl.ds(cols, TILE)] = block
    fetch.wait()


def scaled_update(core, mine, other, peak, x, kv_weight):
    rows, cols = x.shape
    square = (rows, rows)
    return pl.pallas_call(
        functools.partial(
            update_kernel, 0.2 * math.sqrt(max(LATENT, KV_OUT)), 1024, kv_weight.shape[1]
        ),
        out_shape=(
            jax.ShapeDtypeStruct((rows, cols + TILE), bf16),
            jax.ShapeDtypeStruct(kv_weight.shape, bf16),
        ),
        in_specs=[SMEM, VMEM, VMEM, VMEM, VMEM, HBM],
        out_specs=(VMEM, VMEM),
        scratch_shapes=[pltpu.VMEM(square, f32)] * 3
        + [pltpu.VMEM(square, bf16)] * 6
        + [pltpu.SemaphoreType.DMA],
        compiler_params=pltpu.CompilerParams(vmem_limit_bytes=36 * MIB),
        cost_estimate=pl.CostEstimate(
            flops=34 * rows**3 + 2 * rows * rows * cols,
            bytes_accessed=rows * cols * 4,
            transcendentals=0,
        ),
    )(core, mine, other, peak, x, kv_weight)


def gram_sum(core, x, peaks):
    other_core = [(i, i ^ 1) for i in range(4)]
    other_chip = [(i, i ^ 2) for i in range(4)]
    given = lax.ppermute(gram_half(False, core, x), "tensor", other_core)
    mine = gram_half(True, core, x) + given
    mine, peaks = lax.optimization_barrier((mine, peaks))
    peaks = jnp.pad(peaks, ((0, 0), (0, TILE - peaks.shape[1])))
    mine = mine + lax.ppermute(mine, "tensor", other_chip)
    mine, peaks = lax.optimization_barrier((mine, peaks))
    return mine, lax.ppermute(mine, "tensor", other_core), peaks


def step_kernel(weight_ref, recv_ref, update_hbm, new_ref, factor_ref, update_sem):
    step = pl.program_id(0)
    layers, rows, cols = weight_ref.shape
    group = new_ref.shape[0]
    store = pltpu.make_async_copy(recv_ref.at[:, :, pl.ds(0, cols)], update_hbm, update_sem)

    @pl.when(step == 0)
    def _():
        store.start()
        parts = recv_ref[:, :, pl.ds(cols, TILE)].astype(f32)
        peak = None
        for i in range(layers):
            high = parts[i]
            joined = high + pltpu.roll(high, TILE - 32, 1) + pltpu.roll(high, TILE - 64, 1)
            peak = joined if peak is None else jnp.maximum(peak, joined)
        factor_ref[...] = jnp.sqrt(jnp.minimum(1.0, clip_limit / peak))

    heads = cols // (2 * TILE)
    lane = lax.broadcasted_iota(jnp.int32, factor_ref.shape, 1)
    for i in range(group):
        layer = step * group + i
        factors = jnp.sum(jnp.where(lane == layer, factor_ref[...], 0.0), axis=1, keepdims=True)
        for head in range(heads):
            for part in range(2):
                at = pl.ds((2 * head + part) * TILE, TILE)
                stepped = weight_ref[layer, :, at].astype(f32) * (
                    1.0 - learn_rate * weight_decay
                ) - learn_rate * recv_ref[layer, :, at].astype(f32)
                if part == 0:
                    stepped = factors[head : head + 1, :] * stepped
                new_ref[i, :, at] = stepped.astype(bf16)

    @pl.when(step == pl.num_programs(0) - 1)
    def _():
        store.wait()


def apply_step(kv_weight, received):
    layers, rows, cols = kv_weight.shape
    group = layers // 4
    shape = jax.ShapeDtypeStruct(kv_weight.shape, bf16)
    return pl.pallas_call(
        step_kernel,
        grid=(layers // group,),
        out_shape=(shape, shape),
        in_specs=[VMEM, VMEM],
        out_specs=(
            pl.BlockSpec(memory_space=pl.ANY),
            pl.BlockSpec((group, rows, cols), lambda i: (i, 0, 0)),
        ),
        scratch_shapes=[pltpu.VMEM((rows, TILE), f32), pltpu.SemaphoreType.DMA],
        compiler_params=pltpu.CompilerParams(vmem_limit_bytes=24 * MIB),
        cost_estimate=pl.CostEstimate(
            flops=4 * layers * rows * cols, bytes_accessed=8 * layers * rows * cols, transcendentals=0
        ),
    )(kv_weight, received)


def on_device(kv_weight, momentum, gradient, head_counts, logit_peaks):
    layers, rows, shard_width = momentum.shape
    heads_here = shard_width // (KEY_DIM + VALUE_DIM)
    tensor_index = lax.axis_index("tensor")
    core = (tensor_index % 2).astype(jnp.int32).reshape(1)
    head_of = tensor_index * heads_here + lax.broadcasted_iota(
        jnp.int32, momentum.shape, 2
    ) // (KEY_DIM + VALUE_DIM)
    live_mask = (head_of < head_counts[:, None, None]).astype(f32)
    new_momentum = (
        live_mask
        * (momentum_decay * momentum.astype(f32) + gradient.astype(f32))
    ).astype(bf16)
    new_momentum, core = lax.optimization_barrier((new_momentum, core))
    owned = lax.all_to_all(new_momentum, "dp", split_axis=0, concat_axis=0, tiled=True)
    owned = owned.reshape(layers * rows, shard_width)
    mine, other, peaks = gram_sum(core, owned, logit_peaks[:, 0, :].T)
    owned_update, weight = scaled_update(
        core, mine, other, peaks, owned, kv_weight
    )
    received = lax.all_to_all(
        owned_update.reshape(layers, rows, shard_width + TILE),
        "dp",
        split_axis=0,
        concat_axis=0,
        tiled=True,
    )
    update, new_weight = apply_step(weight, received)
    return (update, new_weight, new_momentum)


def solution(mesh):
    placed = (
        P(None, "dp", "tensor"),
        P(None, "dp", "tensor"),
        P(None, "dp", "tensor"),
        P(),
        P(None, "dp", "tensor"),
    )
    return jax.shard_map(
        on_device,
        mesh=mesh,
        in_specs=placed,
        out_specs=(P(None, "dp", "tensor"), P(None, "dp", "tensor"), P(None, "dp", "tensor")),
        check_vma=False,
    )
```

```python
import functools
import math

import jax
import jax.numpy as jnp
from jax import lax
from jax.experimental import pallas as pl
from jax.experimental.pallas import tpu as pltpu
from jax.sharding import PartitionSpec as P

LATENT = 512
KEY_DIM = 128
VALUE_DIM = 128
ITERS = 5
KV_OUT = 16384


momentum_decay = 0.95
first_coef = 3.4445
second_coef = -4.775
third_coef = 2.0315
epsilon = 1e-07
clip_limit = 100.0
learn_rate = 0.02
weight_decay = 0.1

f32 = jnp.float32
bf16 = jnp.bfloat16
MIB = 2**20
TILE = 128
GR = 256
HALF = 4 * TILE + 8
VMEM = pl.BlockSpec(memory_space=pltpu.VMEM)
SMEM = pl.BlockSpec(memory_space=pltpu.SMEM)
HBM = pl.BlockSpec(memory_space=pltpu.HBM)


def dot(left, right):
    return jnp.dot(left, right, preferred_element_type=f32)


def dot_nt(left, right):
    return lax.dot_general(left, right, (((1,), (1,)), ((), ())), preferred_element_type=f32)


def eye_tile():
    shape = (TILE, TILE)
    return lax.broadcasted_iota(jnp.int32, shape, 0) == lax.broadcasted_iota(jnp.int32, shape, 1)


def tiles_of(ref):
    return [pl.ds(i * TILE, TILE) for i in range(ref.shape[0] // TILE)]


def pack_half(half_ref, square, across):
    row = lax.broadcasted_iota(jnp.int32, (TILE, TILE), 0)
    col = lax.broadcasted_iota(jnp.int32, (TILE, TILE), 1)
    first, second = square[:TILE, :TILE], square[TILE:, TILE:]
    half_ref[pl.ds(0, TILE), :] = jnp.where(row <= col, first, second)
    half_ref[pl.ds(TILE, TILE), :] = square[:TILE, TILE:]
    half_ref[pl.ds(2 * TILE, TILE), :] = across[:, :TILE]
    half_ref[pl.ds(3 * TILE, TILE), :] = across[:, TILE:]
    diagonal = jnp.sum(jnp.where(row == col, second, 0.0), axis=0, keepdims=True)
    half_ref[pl.ds(4 * TILE, 8), :] = jnp.broadcast_to(diagonal, (8, TILE))


def unpack_half(half_ref, gram, which):
    row = lax.broadcasted_iota(jnp.int32, (TILE, TILE), 0)
    col = lax.broadcasted_iota(jnp.int32, (TILE, TILE), 1)

    def put(i, j, tile):
        gram[pl.ds(i * TILE, TILE), pl.ds(j * TILE, TILE)] = tile

    both = half_ref[pl.ds(0, TILE), :]
    turned = both.T
    base = 2 * which
    put(base, base, jnp.where(row <= col, both, turned))
    second = jnp.where(row > col, both, turned)
    put(base + 1, base + 1, jnp.where(row == col, half_ref[pl.ds(4 * TILE, 1), :], second))
    for k, (i, j) in enumerate(((base, base + 1), (which, 2), (which, 3))):
        tile = half_ref[pl.ds((k + 1) * TILE, TILE), :]
        put(i, j, tile)
        put(j, i, tile.T)


def gram_kernel(own, core_ref, x_ref, half_ref):
    for which in range(2):

        @pl.when(core_ref[0] == (which if own else 1 - which))
        def _():
            block = x_ref[pl.ds(which * GR, GR), :]
            band = x_ref[pl.ds(which * TILE, TILE), :]
            pack_half(half_ref, dot_nt(block, block), dot_nt(band, x_ref[pl.ds(GR, GR), :]))


def gram_half(own, core, x):
    rows, cols = x.shape
    return pl.pallas_call(
        functools.partial(gram_kernel, own),
        out_shape=jax.ShapeDtypeStruct((HALF, TILE), f32),
        in_specs=[SMEM, VMEM],
        out_specs=VMEM,
        compiler_params=pltpu.CompilerParams(vmem_limit_bytes=32 * MIB),
        cost_estimate=pl.CostEstimate(
            flops=rows * rows * cols * 3 // 4, bytes_accessed=rows * cols * 2, transcendentals=0
        ),
    )(core, x)


def to_col(row):
    tiles = [row[:, i : i + TILE] for i in range(0, row.shape[1], TILE)]
    return jnp.concatenate([jnp.broadcast_to(t, (8, TILE)).T[:, 0:1] for t in tiles], 0)


def settle(value, extra, full_ref, off_ref):
    eye = eye_tile()
    kind = full_ref.dtype
    full_ref[...] = value.astype(kind)
    off_ref[...] = value.astype(bf16)
    found = []
    for i in range(0, value.shape[0], TILE):
        at = pl.ds(i, TILE)
        tile = value[i : i + TILE, i : i + TILE]
        row = jnp.sum(jnp.where(eye, tile, 0.0), axis=0, keepdims=True)
        if extra is not None:
            row = row - extra[:, i : i + TILE]
        if kind != f32:
            row = row.astype(kind).astype(f32)
        full_ref[at, at] = jnp.where(eye, row, tile).astype(kind)
        off_ref[at, at] = jnp.where(eye, 0.0, tile).astype(bf16)
        found.append(row)
    return jnp.concatenate(found, 1)


def newton_schulz(gram, half, total, poly, gram_off, half_off, total_off, poly_off):
    eye = eye_tile()
    trace = 0.0
    for at in tiles_of(gram):
        trace = trace + jnp.sum(jnp.where(eye, gram[at, at], 0.0))
    scale = 1.0 / (jnp.sqrt(trace) + epsilon)
    g_row = settle(gram[...] * scale * scale, None, gram, gram_off)
    for iteration in range(ITERS):
        g_col = to_col(g_row)
        square = third_coef * dot(gram_off[...], gram_off[...])
        p_row = settle(
            square + gram[...] * (second_coef + third_coef * (g_col + g_row)),
            third_coef * g_row * g_row,
            poly,
            poly_off,
        )
        p_col = to_col(p_row)
        if iteration < ITERS - 1:
            h_row = settle(
                dot(poly_off[...], gram_off[...])
                + (first_coef + p_col) * gram[...]
                + poly[...].astype(f32) * g_row,
                p_row * g_row,
                half,
                half_off,
            )
        if iteration == 0:
            t_row = settle(poly[...].astype(f32), jnp.full_like(p_row, -first_coef), total, total_off)
        else:
            t_row = settle(
                dot(poly_off[...], total_off[...])
                + (first_coef + p_col) * total[...]
                + poly[...].astype(f32) * t_row,
                p_row * t_row,
                total,
                total_off,
            )
        if iteration < ITERS - 1:
            g_row = settle(
                dot(half_off[...], poly_off[...])
                + half[...] * (first_coef + p_row)
                + to_col(h_row) * poly[...].astype(f32),
                h_row * p_row,
                gram,
                gram_off,
            )
    return scale


def peak_block(peak):
    high = peak.astype(bf16).astype(f32)
    rest = peak - high
    middle = rest.astype(bf16).astype(f32)
    low = (rest - middle).astype(bf16).astype(f32)
    return (high + pltpu.roll(middle, 32, 1) + pltpu.roll(low, 64, 1)).astype(bf16)


def update_kernel(
    update_scale, width, rows_here,
    core_ref, mine_ref, other_ref, peak_ref, x_ref, weight_hbm, out_ref, weight_ref,
    gram, half, total, poly, gram_off, half_off, total_off, poly_off, factors, weight_sem,
):
    fetch = pltpu.make_async_copy(weight_hbm, weight_ref, weight_sem)
    fetch.start()
    for core, halves in enumerate(((mine_ref, other_ref), (other_ref, mine_ref))):

        @pl.when(core_ref[0] == core)
        def _():
            for which, half_ref in enumerate(halves):
                unpack_half(half_ref, gram, which)

    scale = newton_schulz(
        gram, half, total, poly, gram_off, half_off, total_off, poly_off
    )
    factors[...] = (total[...] * scale).astype(bf16)
    rows, cols = x_ref.shape

    for start in range(0, cols, width):
        at = pl.ds(start, width)
        ortho = dot(factors[...], x_ref[:, at]).astype(bf16)
        out_ref[:, at] = (update_scale * ortho.astype(f32)).astype(bf16)

    block = peak_block(peak_ref[...])
    for i in range(rows // rows_here):
        out_ref[pl.ds(i * rows_here, rows_here), pl.ds(cols, TILE)] = block
    fetch.wait()


def scaled_update(core, mine, other, peak, x, kv_weight):
    rows, cols = x.shape
    square = (rows, rows)
    return pl.pallas_call(
        functools.partial(
            update_kernel, 0.2 * math.sqrt(max(LATENT, KV_OUT)), 1024, kv_weight.shape[1]
        ),
        out_shape=(
            jax.ShapeDtypeStruct((rows, cols + TILE), bf16),
            jax.ShapeDtypeStruct(kv_weight.shape, bf16),
        ),
        in_specs=[SMEM, VMEM, VMEM, VMEM, VMEM, HBM],
        out_specs=(VMEM, VMEM),
        scratch_shapes=[pltpu.VMEM(square, f32)] * 3
        + [pltpu.VMEM(square, bf16)] * 6
        + [pltpu.SemaphoreType.DMA],
        compiler_params=pltpu.CompilerParams(vmem_limit_bytes=36 * MIB),
        cost_estimate=pl.CostEstimate(
            flops=34 * rows**3 + 2 * rows * rows * cols,
            bytes_accessed=rows * cols * 4,
            transcendentals=0,
        ),
    )(core, mine, other, peak, x, kv_weight)


def gram_sum(core, x, peaks):
    other_core = [(i, i ^ 1) for i in range(4)]
    other_chip = [(i, i ^ 2) for i in range(4)]
    given = lax.ppermute(gram_half(False, core, x), "tensor", other_core)
    mine = gram_half(True, core, x) + given
    mine, peaks = lax.optimization_barrier((mine, peaks))
    peaks = jnp.pad(peaks, ((0, 0), (0, TILE - peaks.shape[1])))
    mine = mine + lax.ppermute(mine, "tensor", other_chip)
    mine, peaks = lax.optimization_barrier((mine, peaks))
    return mine, lax.ppermute(mine, "tensor", other_core), peaks


def step_kernel(weight_ref, recv_ref, update_hbm, new_ref, factor_ref, update_sem):
    step = pl.program_id(0)
    layers, rows, cols = weight_ref.shape
    group = new_ref.shape[0]
    store = pltpu.make_async_copy(recv_ref.at[:, :, pl.ds(0, cols)], update_hbm, update_sem)

    @pl.when(step == 0)
    def _():
        store.start()
        parts = recv_ref[:, :, pl.ds(cols, TILE)].astype(f32)
        peak = None
        for i in range(layers):
            high = parts[i]
            joined = high + pltpu.roll(high, TILE - 32, 1) + pltpu.roll(high, TILE - 64, 1)
            peak = joined if peak is None else jnp.maximum(peak, joined)
        factor_ref[...] = jnp.sqrt(jnp.minimum(1.0, clip_limit / peak))

    heads = cols // (2 * TILE)
    lane = lax.broadcasted_iota(jnp.int32, factor_ref.shape, 1)
    for i in range(group):
        layer = step * group + i
        factors = jnp.sum(jnp.where(lane == layer, factor_ref[...], 0.0), axis=1, keepdims=True)
        for head in range(heads):
            for part in range(2):
                at = pl.ds((2 * head + part) * TILE, TILE)
                stepped = weight_ref[layer, :, at].astype(f32) * (
                    1.0 - learn_rate * weight_decay
                ) - learn_rate * recv_ref[layer, :, at].astype(f32)
                if part == 0:
                    stepped = factors[head : head + 1, :] * stepped
                new_ref[i, :, at] = stepped.astype(bf16)

    @pl.when(step == pl.num_programs(0) - 1)
    def _():
        store.wait()


def apply_step(kv_weight, received):
    layers, rows, cols = kv_weight.shape
    group = layers // 2
    shape = jax.ShapeDtypeStruct(kv_weight.shape, bf16)
    return pl.pallas_call(
        step_kernel,
        grid=(layers // group,),
        out_shape=(shape, shape),
        in_specs=[VMEM, VMEM],
        out_specs=(
            pl.BlockSpec(memory_space=pl.ANY),
            pl.BlockSpec((group, rows, cols), lambda i: (i, 0, 0)),
        ),
        scratch_shapes=[pltpu.VMEM((rows, TILE), f32), pltpu.SemaphoreType.DMA],
        compiler_params=pltpu.CompilerParams(vmem_limit_bytes=24 * MIB),
        cost_estimate=pl.CostEstimate(
            flops=4 * layers * rows * cols, bytes_accessed=8 * layers * rows * cols, transcendentals=0
        ),
    )(kv_weight, received)


def on_device(kv_weight, momentum, gradient, head_counts, logit_peaks):
    layers, rows, shard_width = momentum.shape
    heads_here = shard_width // (KEY_DIM + VALUE_DIM)
    tensor_index = lax.axis_index("tensor")
    core = (tensor_index % 2).astype(jnp.int32).reshape(1)
    head_of = tensor_index * heads_here + lax.broadcasted_iota(
        jnp.int32, momentum.shape, 2
    ) // (KEY_DIM + VALUE_DIM)
    live_mask = (head_of < head_counts[:, None, None]).astype(f32)
    new_momentum = (
        live_mask
        * (momentum_decay * momentum.astype(f32) + gradient.astype(f32))
    ).astype(bf16)
    new_momentum, core = lax.optimization_barrier((new_momentum, core))
    owned = lax.all_to_all(new_momentum, "dp", split_axis=0, concat_axis=0, tiled=True)
    owned = owned.reshape(layers * rows, shard_width)
    mine, other, peaks = gram_sum(core, owned, logit_peaks[:, 0, :].T)
    owned_update, weight = scaled_update(
        core, mine, other, peaks, owned, kv_weight
    )
    received = lax.all_to_all(
        owned_update.reshape(layers, rows, shard_width + TILE),
        "dp",
        split_axis=0,
        concat_axis=0,
        tiled=True,
    )
    update, new_weight = apply_step(weight, received)
    return (update, new_weight, new_momentum)


def solution(mesh):
    placed = (
        P(None, "dp", "tensor"),
        P(None, "dp", "tensor"),
        P(None, "dp", "tensor"),
        P(),
        P(None, "dp", "tensor"),
    )
    return jax.shard_map(
        on_device,
        mesh=mesh,
        in_specs=placed,
        out_specs=(P(None, "dp", "tensor"), P(None, "dp", "tensor"), P(None, "dp", "tensor")),
        check_vma=False,
    )
```
